32 devices in a mesh: lat: 4 (over y, x), lon: 8 (over z, core).
Axes of the slice: x: 2, y: 2, z: 4, core: 2. Of those that a mesh axis runs over, the one named last changes fastest.
Arguments:
- tokens: bfloat16 [96, 64, 256], P('lat', 'lon'), may hold values from -6 to 6
- cotangent: bfloat16 [96, 64, 256], P('lat', 'lon'), may hold values from -6 to 6
- query_weight: bfloat16 [256, 256], replicated, may hold values from -0.375 to 0.375
- key_weight: bfloat16 [256, 256], replicated, may hold values from -0.375 to 0.375
- value_weight: bfloat16 [256, 256], replicated, may hold values from -0.375 to 0.375
- out_weight: bfloat16 [256, 256], replicated, may hold values from -0.375 to 0.375
- norm_gain: float32 [256], replicated, may hold values from 0.5 to 1.5
- logit_scale: float32 [8], replicated, may hold values from 2 to 10
Outputs:
- output: bfloat16 [96, 64, 256], P('lat', 'lon')
- grad_tokens: bfloat16 [96, 64, 256], P('lat', 'lon')
- grad_query: float32 [256, 256], replicated
- grad_key: float32 [256, 256], replicated
- grad_value: float32 [256, 256], replicated
- grad_out: float32 [256, 256], replicated
- grad_gain: float32 [256], replicated
- grad_scale: float32 [8], replicated
The draws below stay inside these ranges and needn't reach their ends.
All inputs are finite; a program needn't handle non-finite values.
Results may differ from the reference program's by a relative error of at most 0.012.
The reference program's roundings to bfloat16 on the way (of `normed`, `values`, `softmax_bf`, `attend`, `attend_grad` and `score_grad_bf`) count: a program that leaves them out, or rounds other values in their place, can miss the bound.
Values may be sent and summed in bfloat16 or wider, within the bound.
A program may use at most 64 MiB of HBM per device.

```python
import math
import jax
import jax.numpy as jnp
from jax import lax

D = 256
HEADS = 8
HD = 32
REACH = 6
TR = 24
NR = 96
NC = 64
N_LAT = 4


def shard_levels(rng, dims, split, least, high):
    def one(dim, parts):
        draws = jax.random.uniform(jax.random.fold_in(jax.random.fold_in(rng, 6), dim), (parts,), jnp.float32, least / len(split), high / len(split))
        return jnp.repeat(jnp.exp(draws), dims[dim] // parts).reshape((-1,) + (1,) * (len(dims) - dim - 1))

    factor_of = one(*split[0])
    for cut in split[1:]:
        factor_of = factor_of * one(*cut)
    return factor_of


def noise(own_key, dims, deviation, bound, cuts=(), kind=jnp.bfloat16):
    loudness = shard_levels(own_key, dims, cuts, -0.22, 0.18) if cuts else 1.0
    values = jax.random.normal(own_key, dims, jnp.float32) * deviation * loudness
    return jnp.minimum(jnp.maximum(values, -bound), bound).astype(kind)


def setup_inputs(seed: int = 0) -> dict:
    keys = jax.random.split(jax.random.key(seed), 9)
    return {
        "tokens": noise(keys[0], (NR, NC, D), 1.0, 6.0, ((0, 4), (1, 8))),
        "cotangent": noise(keys[1], (NR, NC, D), 1.0, 6.0, ((0, 4), (1, 8))),
        "query_weight": noise(keys[2], (D, D), D ** -0.5, 0.375),
        "key_weight": noise(keys[3], (D, D), D ** -0.5, 0.375),
        "value_weight": noise(keys[4], (D, D), D ** -0.5, 0.375),
        "out_weight": noise(keys[5], (D, D), D ** -0.5, 0.375),
        "norm_gain": jnp.clip(1.0 + 0.1 * jax.random.normal(keys[6], (D,), jnp.float32), 0.5, 1.5),
        "logit_scale": jnp.clip(jnp.exp(jax.random.uniform(keys[7], (HEADS,), jnp.float32, math.log(2.0), math.log(10.0))), 2.0, 10.0),
    }


EPS = 1e-05
FLOOR = 0.5

def layer_norm(tokens_f, norm_gain):
    center = lax.optimization_barrier(jnp.mean(tokens_f, axis=-1, keepdims=True))
    shifted = tokens_f - center
    spread = lax.optimization_barrier(jnp.mean(shifted * shifted, axis=-1, keepdims=True))
    return norm_gain * shifted * lax.rsqrt(spread + EPS)

def head_norm(raw_values):
    grouped = raw_values.reshape(raw_values.shape[:-1] + (HEADS, raw_values.shape[-1] // HEADS))
    mean_square = lax.optimization_barrier(jnp.mean(grouped * grouped, axis=-1, keepdims=True)) + FLOOR
    return (grouped * lax.rsqrt(mean_square)).reshape(raw_values.shape)

def head_sums(product):
    return lax.optimization_barrier(jnp.sum(product.reshape(product.shape[:-1] + (HEADS, HD)), axis=-1))

def spread_heads(per_head):
    return jnp.repeat(per_head, HD, axis=-1)

def reference(tokens, cotangent, query_weight, key_weight, value_weight, out_weight, norm_gain, logit_scale):
    span_width = 2 * REACH + 1
    offset_count = span_width * span_width
    tokens_f = tokens.astype(jnp.float32)
    normed = layer_norm(tokens_f, norm_gain).astype(jnp.bfloat16)
    flat_normed = normed.reshape(NR * NC, D)
    query_raw = jnp.dot(flat_normed, query_weight, preferred_element_type=jnp.float32)
    key_raw = jnp.dot(flat_normed, key_weight, preferred_element_type=jnp.float32)
    values = jnp.dot(flat_normed, value_weight, preferred_element_type=jnp.float32).astype(jnp.bfloat16).reshape(NR, NC, D)
    query_unit = head_norm(query_raw).astype(jnp.bfloat16).reshape(NR, NC, D)
    key_unit = head_norm(key_raw).astype(jnp.bfloat16).reshape(NR, NC, D)
    flat_cotangent = cotangent.reshape(NR * NC, D)
    attend_grad = jnp.dot(flat_cotangent, out_weight.T, preferred_element_type=jnp.float32).astype(jnp.bfloat16).reshape(NR, NC, D)
    pad_spec = ((REACH, REACH), (0, 0), (0, 0))
    key_pad = jnp.pad(key_unit, pad_spec)
    value_pad = jnp.pad(values, pad_spec)
    factor = logit_scale / HD
    factor_wide = spread_heads(factor)
    row_ids = jnp.arange(TR, dtype=jnp.int32)
    all_offsets = jnp.arange(offset_count, dtype=jnp.int32)

    def block_step(carried, block_index):
        key_acc, value_acc, scale_acc = carried
        row_start = (block_index * TR).astype(jnp.int32)
        query_block = lax.dynamic_slice_in_dim(query_unit, row_start, TR, 0).astype(jnp.float32)
        grad_block = lax.dynamic_slice_in_dim(attend_grad, row_start, TR, 0).astype(jnp.float32)
        key_slab = lax.dynamic_slice_in_dim(key_pad, row_start, TR + 2 * REACH, 0)
        value_slab = lax.dynamic_slice_in_dim(value_pad, row_start, TR + 2 * REACH, 0)

        def shifted_view(source, offset):
            offset = offset.astype(jnp.int32)
            row_shift = offset // span_width
            col_shift = offset % span_width - REACH
            sliced = lax.dynamic_slice_in_dim(source, row_shift, TR, 0).astype(jnp.float32)
            return jnp.roll(sliced, -col_shift, axis=1)

        def visible_rows(offset):
            target = row_start + row_ids + offset // span_width - REACH
            return ((target >= 0) & (target < NR)).astype(jnp.float32)[:, None, None]

        def dots_at(offset):
            return head_sums(query_block * shifted_view(key_slab, offset))
        raw_dots = lax.map(dots_at, all_offsets)
        visible = lax.map(visible_rows, all_offsets)
        exp_scores = jnp.exp(raw_dots * factor) * visible
        softmax = exp_scores / lax.optimization_barrier(jnp.sum(exp_scores, axis=0, keepdims=True))
        softmax_bf = softmax.astype(jnp.bfloat16)

        def add_value(offset, running):
            offset = offset.astype(jnp.int32)
            weight = spread_heads(softmax_bf[offset].astype(jnp.float32))
            return running + weight * shifted_view(value_slab, offset)
        attend_block = lax.fori_loop(0, offset_count, add_value, jnp.zeros((TR, NC, D), jnp.float32))

        def prob_at(offset):
            return head_sums(grad_block * shifted_view(value_slab, offset))
        prob_grad = lax.map(prob_at, all_offsets)
        score_grad = softmax * (prob_grad - lax.optimization_barrier(jnp.sum(softmax * prob_grad, axis=0, keepdims=True)))
        scale_acc = scale_acc + lax.optimization_barrier(jnp.sum(score_grad * raw_dots, axis=(0, 1, 2))) / HD
        score_grad_bf = score_grad.astype(jnp.bfloat16)

        def add_query(offset, running):
            offset = offset.astype(jnp.int32)
            weight = spread_heads(score_grad_bf[offset].astype(jnp.float32))
            return running + weight * shifted_view(key_slab, offset)
        query_unit_grad = lax.fori_loop(0, offset_count, add_query, jnp.zeros((TR, NC, D), jnp.float32)) * factor_wide

        def add_keys(offset, slabs):
            key_part, value_part = slabs
            offset = offset.astype(jnp.int32)
            row_shift = offset // span_width
            col_shift = offset % span_width - REACH
            key_term = jnp.roll(spread_heads(score_grad_bf[offset].astype(jnp.float32)) * query_block, col_shift, axis=1)
            value_term = jnp.roll(spread_heads(softmax_bf[offset].astype(jnp.float32)) * grad_block, col_shift, axis=1)
            key_part = lax.dynamic_update_slice_in_dim(key_part, lax.dynamic_slice_in_dim(key_part, row_shift, TR, 0) + key_term, row_shift, 0)
            value_part = lax.dynamic_update_slice_in_dim(value_part, lax.dynamic_slice_in_dim(value_part, row_shift, TR, 0) + value_term, row_shift, 0)
            return (key_part, value_part)
        empty_slab = jnp.zeros((TR + 2 * REACH, NC, D), jnp.float32)
        key_part, value_part = lax.fori_loop(0, offset_count, add_keys, (empty_slab, empty_slab))
        key_acc = lax.dynamic_update_slice_in_dim(key_acc, lax.dynamic_slice_in_dim(key_acc, row_start, TR + 2 * REACH, 0) + key_part * factor_wide, row_start, 0)
        value_acc = lax.dynamic_update_slice_in_dim(value_acc, lax.dynamic_slice_in_dim(value_acc, row_start, TR + 2 * REACH, 0) + value_part, row_start, 0)
        return ((key_acc, value_acc, scale_acc), (attend_block.astype(jnp.bfloat16), query_unit_grad))
    empty_acc = jnp.zeros((NR + 2 * REACH, NC, D), jnp.float32)
    initial = (empty_acc, empty_acc, jnp.zeros((HEADS,), jnp.float32))
    final_state, stacked = lax.scan(block_step, initial, jnp.arange(N_LAT, dtype=jnp.int32))
    key_acc, value_acc, grad_scale = final_state
    attend = stacked[0].reshape(NR * NC, D)
    query_unit_grad = stacked[1].reshape(NR * NC, D)
    key_unit_grad = key_acc[REACH:REACH + NR].reshape(NR * NC, D)
    value_grad = value_acc[REACH:REACH + NR].reshape(NR * NC, D)
    output = (tokens_f + jnp.dot(attend, out_weight, preferred_element_type=jnp.float32).reshape(NR, NC, D)).astype(jnp.bfloat16)
    grad_out = jnp.dot(attend.T, flat_cotangent, preferred_element_type=jnp.float32)
    query_grad = jax.vjp(head_norm, query_raw)[1](query_unit_grad)[0]
    key_grad = jax.vjp(head_norm, key_raw)[1](key_unit_grad)[0]
    highest = lax.Precision.HIGHEST
    normed_grad = jnp.dot(query_grad, query_weight.T.astype(jnp.float32), precision=highest)
    normed_grad = normed_grad + jnp.dot(key_grad, key_weight.T.astype(jnp.float32), precision=highest)
    normed_grad = normed_grad + jnp.dot(value_grad, value_weight.T.astype(jnp.float32), precision=highest)
    normed_f = flat_normed.astype(jnp.float32)
    grad_query = jnp.dot(normed_f.T, query_grad, precision=highest)
    grad_key = jnp.dot(normed_f.T, key_grad, precision=highest)
    grad_value = jnp.dot(normed_f.T, value_grad, precision=highest)
    norm_back = jax.vjp(layer_norm, tokens_f, norm_gain)[1]
    token_grad, grad_gain = norm_back(normed_grad.reshape(NR, NC, D))
    grad_tokens = (cotangent.astype(jnp.float32) + token_grad).astype(jnp.bfloat16)
    return (output, grad_tokens, grad_query, grad_key, grad_value, grad_out, grad_gain, grad_scale)
```

```python
import functools

import jax
import jax.numpy as jnp
from jax import lax
from jax.experimental import pallas as pl
from jax.experimental.pallas import tpu as pltpu
from jax.sharding import PartitionSpec as P

HEADS = 8
REACH = 6
EPS = 1e-05
FLOOR = 0.5
BLOCK = 8
MESH = pl.DeviceIdType.MESH
F32 = jnp.float32
BF16 = jnp.bfloat16
OFFSETS = ((0, -1), (0, 1), (-1, 0), (1, 0), (-1, -1), (-1, 1), (1, -1), (1, 1))


def dot_nn(a, b):
    return lax.dot_general(a, b, (((1,), (0,)), ((), ())), preferred_element_type=F32)


def dot_nt(a, b):
    return lax.dot_general(a, b, (((1,), (1,)), ((), ())), preferred_element_type=F32)


def dot_tn(a, b):
    return lax.dot_general(a, b, (((0,), (0,)), ((), ())), preferred_element_type=F32)


def group_mean(x, ones):
    high = x.astype(BF16)
    low = (x - high.astype(F32)).astype(BF16)
    return dot_nn(high, ones) + dot_nn(low, ones)


def kernel(
    dims,
    tok, cot, wq, wk, wv, wo, gain, wide, scale,
    out, gtok, fin_out, small_out,
    win, kbuf, vbuf, kraw, nrm, qu, qraw, ag, qe, ge, sc, dp, pb, db, dk, dv, dq, att,
    wg, ngs, ngo, rback, rcore, s1, rlat, s2, rz, fin, small, smcore, smlat, smz,
    hs, hr, bs, br, cs, cr, ls, lr, zs, zr, gs, gr,
):
    n_lat, n_lon, rows, cols = dims
    nz = n_lon // 2
    count = rows * cols
    halo = REACH * cols
    tall = count + 2 * halo
    feats = tok.shape[1]
    head = feats // HEADS
    nb = BLOCK * cols
    wrows = (BLOCK + 2 * REACH) * cols
    keys = 3 * wrows
    reduce_here = wg.shape[0] % (2 * n_lat * nz * 16) == 0
    a = lax.axis_index("lat")
    b = lax.axis_index("lon")
    core = lax.rem(b, 2)
    z = b // 2
    sibling = (a, b + 1 - 2 * core)

    def lat_peer(j):
        return (lax.rem(a + j, n_lat), b)

    def z_peer(j):
        return (a, lax.rem(z + j, nz) * 2 + core)

    def near(da, db):
        return (lax.rem(a + da + n_lat, n_lat), lax.rem(b + db + n_lon, n_lon))

    peers = [near(*o) for o in OFFSETS]
    if reduce_here:
        peers += [sibling] + [lat_peer(j) for j in range(1, n_lat)] + [z_peer(j) for j in range(1, nz)]
    barrier = pltpu.get_barrier_semaphore()
    for p in peers:
        pl.semaphore_signal(barrier, inc=1, device_id=p, device_id_type=MESH)
    pl.semaphore_wait(barrier, len(peers))

    def send(src, dst, s, r, to):
        c = pltpu.make_async_remote_copy(
            src_ref=src, dst_ref=dst, send_sem=s, recv_sem=r, device_id=to, device_id_type=MESH
        )
        c.start()
        return c

    def strip(da):
        return {0: (0, halo, count), 1: (count - halo, 0, halo), -1: (0, halo + count, halo)}[da]

    halos = []
    for i, (da, d) in enumerate(OFFSETS):
        src, dst, n = strip(da)
        halos.append(
            send(
                tok.at[pl.ds(src, n)], win.at[pl.ds((1 - d) * tall + dst, n)],
                hs.at[i], hr.at[i], near(da, d),
            )
        )

    lane = lax.broadcasted_iota(jnp.int32, (1, feats), 1) // head
    gi = lax.broadcasted_iota(jnp.int32, (feats, feats), 0) // head
    gj = lax.broadcasted_iota(jnp.int32, (feats, feats), 1) // head
    ones = jnp.where(gi == gj, 1.0 / head, 0.0).astype(BF16)

    def norm_parts(x):
        x = x.astype(F32)
        sh = x - jnp.mean(x, axis=-1, keepdims=True)
        rstd = lax.rsqrt(jnp.mean(sh * sh, axis=-1, keepdims=True) + EPS)
        return sh, rstd

    def project(x, lo, n):
        sh, rstd = norm_parts(x)
        nn = (gain[...] * sh * rstd).astype(BF16)
        nrm[pl.ds(lo, n)] = nn
        kr = dot_nn(nn, wk[...])
        kraw[pl.ds(lo, n)] = kr
        kbuf[pl.ds(lo, n)] = (kr * lax.rsqrt(group_mean(kr * kr, ones) + FLOOR)).astype(BF16)
        vbuf[pl.ds(lo, n)] = dot_nn(nn, wv[...]).astype(BF16)

    mine = tall + halo
    project(tok[...], mine, count)
    qr = dot_nn(nrm[pl.ds(mine, count)], wq[...])
    qraw[...] = qr
    qu[...] = (qr * lax.rsqrt(group_mean(qr * qr, ones) + FLOOR)).astype(BF16)
    ag[...] = dot_nt(cot[...], wo[...]).astype(BF16)
    dk[...] = jnp.zeros_like(dk)
    dv[...] = jnp.zeros_like(dv)
    small[...] = jnp.zeros_like(small)
    for c in halos:
        c.wait()
    project(win[pl.ds(0, tall)], 0, tall)
    project(win[pl.ds(2 * tall, tall)], 2 * tall, tall)
    project(win[pl.ds(tall, halo)], tall, halo)
    project(win[pl.ds(tall + halo + count, halo)], tall + halo + count, halo)

    total_rows = n_lat * rows
    qi = lax.broadcasted_iota(jnp.int32, (nb, keys), 0)
    ki = lax.broadcasted_iota(jnp.int32, (nb, keys), 1)
    tile = (ki >= wrows).astype(jnp.int32) + (ki >= 2 * wrows).astype(jnp.int32)
    within = ki - tile * wrows
    row_gap = within // cols - REACH - qi // cols
    col_gap = lax.rem(within, cols) + tile * cols - cols - lax.rem(qi, cols)
    close = (jnp.abs(row_gap) <= REACH) & (jnp.abs(col_gap) <= REACH)
    krow = within // cols - REACH + a * rows

    def block(i, carried):
        q0 = pl.multiple_of(i * nb, nb)
        qb = qu[pl.ds(q0, nb)]
        gb = ag[pl.ds(q0, nb)]
        for h in range(HEADS):
            qe[pl.ds(h * nb, nb)] = jnp.where(lane == h, qb, jnp.zeros_like(qb))
            ge[pl.ds(h * nb, nb)] = jnp.where(lane == h, gb, jnp.zeros_like(gb))
        starts = [pl.multiple_of(t * tall + i * nb, 16) for t in range(3)]
        kw = jnp.concatenate([kbuf[pl.ds(s, wrows)] for s in starts], axis=0)
        vw = jnp.concatenate([vbuf[pl.ds(s, wrows)] for s in starts], axis=0)
        sc[...] = dot_nt(qe[...], kw)
        dp[...] = dot_nt(ge[...], vw)
        gr_row = krow + i * BLOCK
        seen = jnp.where(close & (gr_row >= 0) & (gr_row < total_rows), 1.0, 0.0)
        for h in range(HEADS):
            part = pl.ds(h * nb, nb)
            s = sc[part]
            e = jnp.exp(s * scale[h]) * seen
            p = e * (1.0 / jnp.sum(e, axis=1, keepdims=True))
            pb[part] = p.astype(BF16)
            t = dp[part]
            g = p * (t - jnp.sum(p * t, axis=1, keepdims=True))
            db[part] = g.astype(BF16)
            tot = jnp.sum(jnp.sum(g * s, axis=1, keepdims=True), axis=0, keepdims=True)
            small[1:2, :] = small[1:2, :] + jnp.where(lane == h, tot * (1.0 / head), 0.0)
        o = dot_nn(pb[...], vw)
        u = dot_nn(db[...], kw)
        oa = jnp.zeros((nb, feats), F32)
        ua = jnp.zeros((nb, feats), F32)
        for h in range(HEADS):
            oa = jnp.where(lane == h, o[h * nb : (h + 1) * nb], oa)
            ua = jnp.where(lane == h, u[h * nb : (h + 1) * nb], ua)
        att[pl.ds(q0, nb)] = oa.astype(BF16)
        dq[pl.ds(q0, nb)] = ua
        kg = dot_tn(db[...], qe[...])
        vg = dot_tn(pb[...], ge[...])
        for t in range(3):
            part = pl.ds(starts[t], wrows)
            dk[part] = dk[part] + kg[t * wrows : (t + 1) * wrows]
            dv[part] = dv[part] + vg[t * wrows : (t + 1) * wrows]
        return carried

    lax.fori_loop(0, rows // BLOCK, block, 0)

    def head_back(raw, g):
        s = lax.rsqrt(group_mean(raw * raw, ones) + FLOOR)
        return s * g - raw * (s * s * s) * group_mean(g * raw, ones)

    dqr = head_back(qraw[...], dq[...] * wide[...]).astype(BF16)
    dkr = head_back(kraw[...], dk[...] * wide[...]).astype(BF16)
    dvb = dv[...].astype(BF16)
    wg[pl.ds(0, feats)] = dot_tn(nrm[pl.ds(mine, count)], dqr).astype(BF16)
    wg[pl.ds(feats, feats)] = dot_tn(nrm[...], dkr).astype(BF16)
    wg[pl.ds(2 * feats, feats)] = dot_tn(nrm[...], dvb).astype(BF16)
    wg[pl.ds(3 * feats, feats)] = dot_tn(att[...], cot[...]).astype(BF16)
    pending = []
    if reduce_here:
        half = wg.shape[0] // 2
        quarter = half // n_lat
        last = quarter // nz
        my_half = pl.multiple_of(core * half, 16)
        other = pl.multiple_of((1 - core) * half, 16)
        c_core = send(wg.at[pl.ds(other, half)], rcore, cs.at[0], cr.at[0], sibling)

    ng = dot_nt(dkr, wk[...]) + dot_nt(dvb, wv[...])
    ngs[...] = ng.astype(BF16)
    backs = []
    for i, (da, d) in enumerate(OFFSETS):
        _, _, n = strip(da)
        src = {0: halo, -1: 0, 1: halo + count}[da]
        backs.append(
            send(
                ngs.at[pl.ds((1 + d) * tall + src, n)], rback.at[i, pl.ds(0, n)],
                bs.at[i], br.at[i], near(da, d),
            )
        )
    own = ng[mine : mine + count] + dot_nt(dqr, wq[...])
    ngo[...] = own
    gsum = jnp.zeros((1, feats), F32)
    for lo, n in ((0, tall), (2 * tall, tall), (tall, halo), (mine + count, halo)):
        sh, rstd = norm_parts(win[pl.ds(lo, n)])
        gsum = gsum + jnp.sum(ng[lo : lo + n] * (sh * rstd), axis=0, keepdims=True)
    sh, rstd = norm_parts(tok[...])
    gsum = gsum + jnp.sum(own * (sh * rstd), axis=0, keepdims=True)
    small[0:1, :] = gsum

    if reduce_here:
        m_core = send(small, smcore, cs.at[1], cr.at[1], sibling)
        c_core.wait()
        s1[...] = (wg[pl.ds(my_half, half)].astype(F32) + rcore[...].astype(F32)).astype(BF16)
        c_lat = []
        for j in range(1, n_lat):
            to = lat_peer(j)
            lo = pl.multiple_of(to[0] * quarter, 16)
            c_lat.append(send(s1.at[pl.ds(lo, quarter)], rlat.at[j - 1], ls.at[j], lr.at[j], to))
        m_core.wait()
        smlat[pl.ds(a, 1)] = (small[...] + smcore[...])[None]
        m_lat = [
            send(smlat.at[a], smlat.at[a], ls.at[n_lat + j], lr.at[n_lat + j], lat_peer(j))
            for j in range(1, n_lat)
        ]

    out[...] = (tok[...].astype(F32) + dot_nn(att[...], wo[...])).astype(BF16)
    for c in backs:
        c.wait()
    ngo[...] = ngo[...] + rback[0].astype(F32) + rback[1].astype(F32)
    for da, lo in ((-1, 0), (1, count - halo)):
        part = pl.ds(lo, halo)
        add = ngo[part]
        for i, o in enumerate(OFFSETS):
            if o[0] == -da:
                add = add + rback[i, pl.ds(0, halo)].astype(F32)
        ngo[part] = add
    sh, rstd = norm_parts(tok[...])
    xhat = sh * rstd
    g = ngo[...] * gain[...]
    tg = rstd * (
        g - jnp.mean(g, axis=-1, keepdims=True) - xhat * jnp.mean(g * xhat, axis=-1, keepdims=True)
    )
    gtok[...] = (cot[...].astype(F32) + tg).astype(BF16)

    if reduce_here:
        for c in c_lat:
            c.wait()
        acc = s1[pl.ds(pl.multiple_of(a * quarter, 16), quarter)].astype(F32)
        for j in range(1, n_lat):
            acc = acc + rlat[j - 1].astype(F32)
        s2[...] = acc.astype(BF16)
        c_z = []
        for j in range(1, nz):
            to = z_peer(j)
            lo = pl.multiple_of((to[1] // 2) * last, 16)
            c_z.append(send(s2.at[pl.ds(lo, last)], rz.at[j - 1], zs.at[j], zr.at[j], to))
        for c in m_lat:
            c.wait()
        acc = smlat[0]
        for j in range(1, n_lat):
            acc = acc + smlat[j]
        smz[pl.ds(z, 1)] = acc[None]
        m_z = [
            send(smz.at[z], smz.at[z], zs.at[nz + j], zr.at[nz + j], z_peer(j)) for j in range(1, nz)
        ]
        for c in c_z:
            c.wait()
        acc = s2[pl.ds(pl.multiple_of(z * last, 16), last)].astype(F32)
        for j in range(1, nz):
            acc = acc + rz[j - 1].astype(F32)
        block_lo = pl.multiple_of(my_half + a * quarter, 16)
        leaf = pl.ds(pl.multiple_of(block_lo + z * last, 16), last)
        fin[leaf] = acc.astype(BF16)
        c_z = [send(fin.at[leaf], fin.at[leaf], gs.at[j], gr.at[j], z_peer(j)) for j in range(1, nz)]
        for c in m_z:
            c.wait()
        acc = smz[0]
        for j in range(1, nz):
            acc = acc + smz[j]
        small_out[...] = acc
        for c in c_z:
            c.wait()
        mid = pl.ds(block_lo, quarter)
        c_lat = [
            send(fin.at[mid], fin.at[mid], gs.at[nz + j], gr.at[nz + j], lat_peer(j))
            for j in range(1, n_lat)
        ]
        for c in c_lat:
            c.wait()
        top = pl.ds(my_half, half)
        send(fin.at[top], fin.at[top], gs.at[0], gr.at[0], sibling).wait()
        fin_out[...] = fin[...]
    else:
        fin_out[...] = wg[...]
        small_out[...] = small[...]


def local(dims, tokens, cotangent, wq, wk, wv, wo, norm_gain, logit_scale):
    n_lat, n_lon, rows, cols = dims
    nz = n_lon // 2
    feats = tokens.shape[-1]
    head = feats // HEADS
    count = rows * cols
    halo = REACH * cols
    window = 3 * (count + 2 * halo)
    nb = BLOCK * cols * HEADS
    keys = 3 * (BLOCK + 2 * REACH) * cols
    reduce_here = 4 * feats % (2 * n_lat * nz * 16) == 0
    half = 2 * feats
    quarter = max(16, half // n_lat) if reduce_here else 16
    last = quarter // nz if reduce_here else 16
    pl_lat = n_lat if reduce_here else 2
    pl_z = nz if reduce_here else 2
    vm = pl.BlockSpec(memory_space=pltpu.VMEM)
    sm = pl.BlockSpec(memory_space=pltpu.SMEM)
    dma = pltpu.SemaphoreType.DMA
    factor = logit_scale / head
    V = pltpu.VMEM
    scratch = [
        V((window, feats), BF16), V((window, feats), BF16), V((window, feats), BF16),
        V((window, feats), F32), V((window, feats), BF16),
        V((count, feats), BF16), V((count, feats), F32), V((count, feats), BF16),
        V((nb, feats), BF16), V((nb, feats), BF16),
        V((nb, keys), F32), V((nb, keys), F32), V((nb, keys), BF16), V((nb, keys), BF16),
        V((window, feats), F32), V((window, feats), F32), V((count, feats), F32),
        V((count, feats), BF16),
        V((4 * feats, feats), BF16), V((window, feats), BF16), V((count, feats), F32),
        V((8, count, feats), BF16),
        V((half, feats), BF16), V((half, feats), BF16),
        V((pl_lat - 1, quarter, feats), BF16), V((quarter, feats), BF16),
        V((pl_z - 1, last, feats), BF16), V((4 * feats, feats), BF16),
        V((8, feats), F32), V((8, feats), F32), V((pl_lat, 8, feats), F32), V((pl_z, 8, feats), F32),
        dma((8,)), dma((8,)), dma((8,)), dma((8,)), dma((2,)), dma((2,)),
        dma((2 * pl_lat,)), dma((2 * pl_lat,)), dma((2 * pl_z,)), dma((2 * pl_z,)),
        dma((pl_lat + pl_z,)), dma((pl_lat + pl_z,)),
    ]
    out, gtok, fin, small = pl.pallas_call(
        functools.partial(kernel, dims),
        out_shape=[
            jax.ShapeDtypeStruct((count, feats), BF16),
            jax.ShapeDtypeStruct((count, feats), BF16),
            jax.ShapeDtypeStruct((4 * feats, feats), BF16),
            jax.ShapeDtypeStruct((8, feats), F32),
        ],
        in_specs=[vm] * 8 + [sm],
        out_specs=[vm] * 4,
        scratch_shapes=scratch,
        compiler_params=pltpu.CompilerParams(
            collective_id=0, has_side_effects=True, vmem_limit_bytes=50 * 1024 * 1024
        ),
    )(
        tokens.reshape(count, feats), cotangent.reshape(count, feats), wq, wk, wv, wo,
        norm_gain.reshape(1, feats), jnp.repeat(factor, head).reshape(1, feats), factor,
    )
    fin = fin.astype(F32)
    if not reduce_here:
        fin, small = lax.psum((fin, small), ("lat", "lon"))
    return (
        out.reshape(rows, cols, feats), gtok.reshape(rows, cols, feats),
        fin[:feats], fin[feats : 2 * feats], fin[2 * feats : 3 * feats], fin[3 * feats :],
        small[0], small[1, ::head],
    )


def solution(mesh):
    n_lat, n_lon = mesh.shape["lat"], mesh.shape["lon"]

    def run(tokens, *rest):
        dims = (n_lat, n_lon, tokens.shape[0], tokens.shape[1])
        return local(dims, tokens, *rest)

    return jax.shard_map(
        run,
        mesh=mesh,
        in_specs=(P("lat", "lon", None), P("lat", "lon", None), P(), P(), P(), P(), P(), P()),
        out_specs=(P("lat", "lon", None), P("lat", "lon", None), P(), P(), P(), P(), P(), P()),
        check_vma=False,
    )
```

```python
import functools

import jax
import jax.numpy as jnp
from jax import lax
from jax.experimental import pallas as pl
from jax.experimental.pallas import tpu as pltpu
from jax.sharding import PartitionSpec as P

HEADS = 8
REACH = 6
EPS = 1e-05
FLOOR = 0.5
BLOCK = 8
MESH = pl.DeviceIdType.MESH
F32 = jnp.float32
BF16 = jnp.bfloat16
OFFSETS = ((0, -1), (0, 1), (-1, 0), (1, 0), (-1, -1), (-1, 1), (1, -1), (1, 1))


def dot_nn(a, b):
    return lax.dot_general(a, b, (((1,), (0,)), ((), ())), preferred_element_type=F32)


def dot_nt(a, b):
    return lax.dot_general(a, b, (((1,), (1,)), ((), ())), preferred_element_type=F32)


def dot_tn(a, b):
    return lax.dot_general(a, b, (((0,), (0,)), ((), ())), preferred_element_type=F32)


def group_mean(x, ones):
    return dot_nn(x.astype(BF16), ones)


def kernel(
    dims,
    tok_in, cot_in, wq_in, wk_in, wv_in, wo_in, gain_in, scale,
    out, gtok, fin_out, small_out,
    tok, cot, wq, wk, wv, wo, gain,
    win, kbuf, vbuf, kraw, kinv, xhat, nrm, qu, qraw, qinv, ag, qe, ge, sc, dp, pb, db, dk, dv, dq, att,
    wg, ngs, ngo, rback, rcore, s1, rlat, s2, rz, fin, small, smcore, smlat, smz,
    load_sem, hs, hr, bs, br, cs, cr, ls, lr, zs, zr, gs, gr, ts, tr,
):
    n_lat, n_lon, rows, cols = dims
    nz = n_lon // 2
    count = rows * cols
    halo = REACH * cols
    tall = count + 2 * halo
    feats = tok_in.shape[1]
    head = feats // HEADS
    nb = BLOCK * cols
    wrows = (BLOCK + 2 * REACH) * cols
    keys = 3 * wrows
    reduce_here = 2 * feats % (2 * n_lat * nz * 16) == 0
    a = lax.axis_index("lat")
    b = lax.axis_index("lon")
    core = lax.rem(b, 2)
    z = b // 2
    sibling = (a, b + 1 - 2 * core)

    def lat_peer(j):
        return (lax.rem(a + j, n_lat), b)

    def z_peer(j):
        return (a, lax.rem(z + j, nz) * 2 + core)

    def near(da, db):
        return (lax.rem(a + da + n_lat, n_lat), lax.rem(b + db + n_lon, n_lon))

    peers = [near(*o) for o in OFFSETS]
    if reduce_here:
        peers += [sibling] + [lat_peer(j) for j in range(1, n_lat)] + [z_peer(j) for j in range(1, nz)]
    barrier = pltpu.get_barrier_semaphore()
    for p in peers:
        pl.semaphore_signal(barrier, inc=1, device_id=p, device_id_type=MESH)
    loads = []
    for src, dst in (
        (tok_in, tok), (wk_in, wk), (wv_in, wv), (gain_in, gain), (wq_in, wq), (cot_in, cot), (wo_in, wo)
    ):
        c = pltpu.make_async_copy(src, dst, load_sem.at[len(loads)])
        c.start()
        loads.append(c)
    pl.semaphore_wait(barrier, len(peers))

    def send(src, dst, s, r, to):
        c = pltpu.make_async_remote_copy(
            src_ref=src, dst_ref=dst, send_sem=s, recv_sem=r, device_id=to, device_id_type=MESH
        )
        c.start()
        return c

    def strip(da):
        return {0: (0, halo, count), 1: (count - halo, 0, halo), -1: (0, halo + count, halo)}[da]

    halos = []
    for i, (da, d) in enumerate(OFFSETS):
        src, dst, n = strip(da)
        halos.append(
            send(
                tok_in.at[pl.ds(src, n)], win.at[pl.ds((1 - d) * tall + dst, n)],
                hs.at[i], hr.at[i], near(da, d),
            )
        )

    lane = lax.broadcasted_iota(jnp.int32, (1, feats), 1) // head
    gi = lax.broadcasted_iota(jnp.int32, (feats, feats), 0) // head
    gj = lax.broadcasted_iota(jnp.int32, (feats, feats), 1) // head
    ones = jnp.where(gi == gj, 1.0 / head, 0.0).astype(BF16)

    def norm_parts(x):
        x = x.astype(F32)
        sh = x - jnp.mean(x, axis=-1, keepdims=True)
        rstd = lax.rsqrt(jnp.mean(sh * sh, axis=-1, keepdims=True) + EPS)
        return sh, rstd

    def project(x, lo, n):
        sh, rstd = norm_parts(x)
        xh = sh * rstd
        xhat[pl.ds(lo, n)] = xh
        nn = (gain[...] * xh).astype(BF16)
        nrm[pl.ds(lo, n)] = nn
        kr = dot_nn(nn, wk[...])
        kraw[pl.ds(lo, n)] = kr
        inv = lax.rsqrt(group_mean(kr * kr, ones) + FLOOR)
        kinv[pl.ds(lo, n)] = inv
        kbuf[pl.ds(lo, n)] = (kr * inv).astype(BF16)
        vbuf[pl.ds(lo, n)] = dot_nn(nn, wv[...]).astype(BF16)

    mine = tall + halo
    wide = jnp.zeros((1, feats), F32)
    for h in range(HEADS):
        wide = jnp.where(lane == h, scale[h] * (1.0 / head), wide)
    for c in loads:
        c.wait()
    project(tok[...], mine, count)
    qr = dot_nn(nrm[pl.ds(mine, count)], wq[...])
    qraw[...] = qr
    inv = lax.rsqrt(group_mean(qr * qr, ones) + FLOOR)
    qinv[...] = inv
    qu[...] = (qr * inv).astype(BF16)
    ag[...] = dot_nt(cot[...], wo[...]).astype(BF16)
    dk[...] = jnp.zeros_like(dk)
    dv[...] = jnp.zeros_like(dv)
    small[...] = jnp.zeros_like(small)
    for c in halos:
        c.wait()
    project(win[pl.ds(0, tall)], 0, tall)
    project(win[pl.ds(2 * tall, tall)], 2 * tall, tall)
    project(win[pl.ds(tall, halo)], tall, halo)
    project(win[pl.ds(tall + halo + count, halo)], tall + halo + count, halo)

    total_rows = n_lat * rows
    qi = lax.broadcasted_iota(jnp.int32, (nb, keys), 0)
    ki = lax.broadcasted_iota(jnp.int32, (nb, keys), 1)
    tile = (ki >= wrows).astype(jnp.int32) + (ki >= 2 * wrows).astype(jnp.int32)
    within = ki - tile * wrows
    row_gap = within // cols - REACH - qi // cols
    col_gap = lax.rem(within, cols) + tile * cols - cols - lax.rem(qi, cols)
    close = (jnp.abs(row_gap) <= REACH) & (jnp.abs(col_gap) <= REACH)
    krow = within // cols - REACH + a * rows

    def block(i, carried):
        q0 = pl.multiple_of(i * nb, nb)
        qb = qu[pl.ds(q0, nb)]
        gb = ag[pl.ds(q0, nb)]
        for h in range(HEADS):
            qe[pl.ds(h * nb, nb)] = jnp.where(lane == h, qb, jnp.zeros_like(qb))
            ge[pl.ds(h * nb, nb)] = jnp.where(lane == h, gb, jnp.zeros_like(gb))
        starts = [pl.multiple_of(t * tall + i * nb, 16) for t in range(3)]
        kw = jnp.concatenate([kbuf[pl.ds(s, wrows)] for s in starts], axis=0)
        vw = jnp.concatenate([vbuf[pl.ds(s, wrows)] for s in starts], axis=0)
        sc[...] = dot_nt(qe[...], kw)
        dp[...] = dot_nt(ge[...], vw)
        gr_row = krow + i * BLOCK
        seen = jnp.where(close & (gr_row >= 0) & (gr_row < total_rows), 1.0, 0.0)
        for h in range(HEADS):
            part = pl.ds(h * nb, nb)
            s = sc[part]
            e = jnp.exp(s * (scale[h] * (1.0 / head))) * seen
            p = e * (1.0 / jnp.sum(e, axis=1, keepdims=True))
            pb[part] = p.astype(BF16)
            t = dp[part]
            g = p * (t - jnp.sum(p * t, axis=1, keepdims=True))
            db[part] = g.astype(BF16)
            tot = jnp.sum(jnp.sum(g * s, axis=1, keepdims=True), axis=0, keepdims=True)
            small[1:2, :] = small[1:2, :] + jnp.where(lane == h, tot * (1.0 / head), 0.0)
        o = dot_nn(pb[...], vw)
        u = dot_nn(db[...], kw)
        oa = jnp.zeros((nb, feats), F32)
        ua = jnp.zeros((nb, feats), F32)
        for h in range(HEADS):
            oa = jnp.where(lane == h, o[h * nb : (h + 1) * nb], oa)
            ua = jnp.where(lane == h, u[h * nb : (h + 1) * nb], ua)
        att[pl.ds(q0, nb)] = oa.astype(BF16)
        dq[pl.ds(q0, nb)] = ua
        kg = dot_tn(db[...], qe[...])
        vg = dot_tn(pb[...], ge[...])
        for t in range(3):
            part = pl.ds(starts[t], wrows)
            dk[part] = dk[part] + kg[t * wrows : (t + 1) * wrows]
            dv[part] = dv[part] + vg[t * wrows : (t + 1) * wrows]
        return carried

    lax.fori_loop(0, rows // BLOCK, block, 0)

    def head_back(raw, inv, g):
        return inv * (g - raw * (inv * inv) * group_mean(g * raw, ones))

    half, quarter, last = wg.shape[1] // 2, rlat.shape[2], rz.shape[2]
    chunks = range(wg.shape[0])
    my_half = pl.multiple_of(core * half, 16)
    block_lo = pl.multiple_of(my_half + a * quarter, 16)
    leaf_lo = pl.multiple_of(block_lo + z * last, 16)

    def core_send(k):
        lo = pl.multiple_of((1 - core) * half, 16)
        return send(wg.at[k, pl.ds(lo, half)], rcore.at[k], cs.at[k], cr.at[k], sibling)

    def lat_send(k):
        s1[k] = (wg[k, pl.ds(my_half, half)].astype(F32) + rcore[k].astype(F32)).astype(BF16)
        sent = []
        for j in range(1, n_lat):
            to = lat_peer(j)
            lo = pl.multiple_of(to[0] * quarter, 16)
            sent.append(
                send(s1.at[k, pl.ds(lo, quarter)], rlat.at[k, j - 1], ls.at[k, j], lr.at[k, j], to)
            )
        return sent

    def z_send(k):
        acc = s1[k, pl.ds(pl.multiple_of(a * quarter, 16), quarter)].astype(F32)
        for j in range(1, n_lat):
            acc = acc + rlat[k, j - 1].astype(F32)
        s2[k] = acc.astype(BF16)
        sent = []
        for j in range(1, nz):
            to = z_peer(j)
            lo = pl.multiple_of((to[1] // 2) * last, 16)
            sent.append(send(s2.at[k, pl.ds(lo, last)], rz.at[k, j - 1], zs.at[k, j], zr.at[k, j], to))
        return sent

    def z_spread(k):
        acc = s2[k, pl.ds(pl.multiple_of(z * last, 16), last)].astype(F32)
        for j in range(1, nz):
            acc = acc + rz[k, j - 1].astype(F32)
        leaf = pl.ds(leaf_lo, last)
        fin[k, leaf] = acc.astype(BF16)
        return [
            send(fin.at[k, leaf], fin.at[k, leaf], gs.at[k, j], gr.at[k, j], z_peer(j))
            for j in range(1, nz)
        ]

    def lat_spread(k):
        mid = pl.ds(block_lo, quarter)
        return [
            send(fin.at[k, mid], fin.at[k, mid], gs.at[k, nz + j], gr.at[k, nz + j], lat_peer(j))
            for j in range(1, n_lat)
        ]

    def core_spread(k):
        top = pl.ds(my_half, half)
        return [send(fin.at[k, top], fin.at[k, top], gs.at[k, 0], gr.at[k, 0], sibling)]

    def done(copies):
        for c in copies:
            c.wait()

    dqr = head_back(qraw[...], qinv[...], dq[...] * wide).astype(BF16)
    wg[0, pl.ds(0, feats)] = dot_tn(nrm[pl.ds(mine, count)], dqr).astype(BF16)
    wg[0, pl.ds(feats, feats)] = dot_tn(att[...], cot[...]).astype(BF16)
    if reduce_here:
        c0 = [core_send(0)]
    dkr = head_back(kraw[...], kinv[...], dk[...] * wide).astype(BF16)
    dvb = dv[...].astype(BF16)
    wg[1, pl.ds(0, feats)] = dot_tn(nrm[...], dkr).astype(BF16)
    wg[1, pl.ds(feats, feats)] = dot_tn(nrm[...], dvb).astype(BF16)
    if reduce_here:
        c1 = [core_send(1)]
        done(c0)
        c0 = lat_send(0)
    ng = dot_nt(dkr, wk[...]) + dot_nt(dvb, wv[...])
    ngs[...] = ng.astype(BF16)
    backs = []
    for i, (da, d) in enumerate(OFFSETS):
        _, _, n = strip(da)
        src = {0: halo, -1: 0, 1: halo + count}[da]
        backs.append(
            send(
                ngs.at[pl.ds((1 + d) * tall + src, n)], rback.at[i, pl.ds(0, n)],
                bs.at[i], br.at[i], near(da, d),
            )
        )
    if reduce_here:
        done(c1)
        c1 = lat_send(1)
    from_q = dot_nt(dqr, wq[...])
    ngo[...] = ng[mine : mine + count] + from_q
    own_hat = xhat[pl.ds(mine, count)]
    small[0:1, :] = jnp.sum(ng * xhat[...], axis=0, keepdims=True) + jnp.sum(
        from_q * own_hat, axis=0, keepdims=True
    )
    if reduce_here:
        m = [send(small, smcore, ts.at[0], tr.at[0], sibling)]
        done(c0)
        c0 = z_send(0)
        done(m)
        smlat[pl.ds(a, 1)] = (small[...] + smcore[...])[None]
        m = [send(smlat.at[a], smlat.at[a], ts.at[j], tr.at[j], lat_peer(j)) for j in range(1, n_lat)]
    out[...] = (tok[...].astype(F32) + dot_nn(att[...], wo[...])).astype(BF16)
    if reduce_here:
        done(c1)
        c1 = z_send(1)
        done(c0)
        c0 = z_spread(0)
        done(m)
        acc = smlat[0]
        for j in range(1, n_lat):
            acc = acc + smlat[j]
        smz[pl.ds(z, 1)] = acc[None]
        m = [
            send(smz.at[z], smz.at[z], ts.at[n_lat + j], tr.at[n_lat + j], z_peer(j))
            for j in range(1, nz)
        ]
        done(c1)
        c1 = z_spread(1)
        done(c0)
        c0 = lat_spread(0)
        done(c1)
        c1 = lat_spread(1)
    done(backs)
    ngo[...] = ngo[...] + rback[0].astype(F32) + rback[1].astype(F32)
    for da, lo in ((-1, 0), (1, count - halo)):
        part = pl.ds(lo, halo)
        add = ngo[part]
        for i, o in enumerate(OFFSETS):
            if o[0] == -da:
                add = add + rback[i, pl.ds(0, halo)].astype(F32)
        ngo[part] = add
    sh, rstd = norm_parts(tok[...])
    g = ngo[...] * gain[...]
    tg = rstd * (
        g
        - jnp.mean(g, axis=-1, keepdims=True)
        - own_hat * jnp.mean(g * own_hat, axis=-1, keepdims=True)
    )
    gtok[...] = (cot[...].astype(F32) + tg).astype(BF16)
    if reduce_here:
        done(c0)
        c0 = core_spread(0)
        done(c1)
        c1 = core_spread(1)
        done(m)
        acc = smz[0]
        for j in range(1, nz):
            acc = acc + smz[j]
        small_out[...] = acc
        done(c0)
        fin_out[0] = fin[0]
        done(c1)
        fin_out[1] = fin[1]
    else:
        fin_out[...] = wg[...]
        small_out[...] = small[...]


def finish(fin, small, out, gtok, *refs):
    results, staged, sem = refs[:8], refs[8:14], refs[14]
    feats = fin.shape[2]
    pending = []

    def store(src, dst):
        c = pltpu.make_async_copy(src, dst, sem.at[len(pending)])
        c.start()
        pending.append(c)

    store(out, results[0])
    store(gtok, results[1])
    for n, (k, lo) in enumerate(((0, 0), (1, 0), (1, feats), (0, feats))):
        staged[n][...] = fin[k, pl.ds(lo, feats)].astype(F32)
        store(staged[n], results[2 + n])
    staged[4][...] = small[0:1, :]
    store(staged[4], results[6])
    lane = lax.broadcasted_iota(jnp.int32, (feats, HEADS), 0)
    col = lax.broadcasted_iota(jnp.int32, (feats, HEADS), 1)
    pick = jnp.where(lane == col * (feats // HEADS), 1.0, 0.0)
    staged[5][...] = lax.dot_general(
        small[...], pick, (((1,), (0,)), ((), ())), precision=lax.Precision.HIGHEST,
        preferred_element_type=F32,
    )[1:2, :]
    store(staged[5], results[7])
    for c in pending:
        c.wait()


def local(dims, tokens, cotangent, wq, wk, wv, wo, norm_gain, logit_scale):
    n_lat, n_lon, rows, cols = dims
    nz = n_lon // 2
    feats = tokens.shape[-1]
    head = feats // HEADS
    count = rows * cols
    halo = REACH * cols
    window = 3 * (count + 2 * halo)
    nb = BLOCK * cols * HEADS
    keys = 3 * (BLOCK + 2 * REACH) * cols
    reduce_here = 2 * feats % (2 * n_lat * nz * 16) == 0
    half = feats
    quarter = half // n_lat if reduce_here else 16
    last = quarter // nz if reduce_here else 16
    pl_lat = n_lat if reduce_here else 2
    pl_z = nz if reduce_here else 2
    vm = pl.BlockSpec(memory_space=pltpu.VMEM)
    sm = pl.BlockSpec(memory_space=pltpu.SMEM)
    hbm = pl.BlockSpec(memory_space=pltpu.HBM)
    dma = pltpu.SemaphoreType.DMA
    V = pltpu.VMEM
    square = V((feats, feats), BF16)
    scratch = [
        V((count, feats), BF16), V((count, feats), BF16), square, square, square, square,
        V((1, feats), F32),
        V((window, feats), BF16), V((window, feats), BF16), V((window, feats), BF16),
        V((window, feats), F32), V((window, feats), F32), V((window, feats), F32),
        V((window, feats), BF16),
        V((count, feats), BF16), V((count, feats), F32), V((count, feats), F32),
        V((count, feats), BF16),
        V((nb, feats), BF16), V((nb, feats), BF16),
        V((nb, keys), F32), V((nb, keys), F32), V((nb, keys), BF16), V((nb, keys), BF16),
        V((window, feats), F32), V((window, feats), F32), V((count, feats), F32),
        V((count, feats), BF16),
        V((2, 2 * feats, feats), BF16), V((window, feats), BF16), V((count, feats), F32),
        V((8, count, feats), BF16),
        V((2, half, feats), BF16), V((2, half, feats), BF16),
        V((2, pl_lat - 1, quarter, feats), BF16), V((2, quarter, feats), BF16),
        V((2, pl_z - 1, last, feats), BF16), V((2, 2 * feats, feats), BF16),
        V((8, feats), F32), V((8, feats), F32), V((pl_lat, 8, feats), F32), V((pl_z, 8, feats), F32),
        dma((7,)),
        dma((8,)), dma((8,)), dma((8,)), dma((8,)), dma((2,)), dma((2,)),
        dma((2, pl_lat)), dma((2, pl_lat)), dma((2, pl_z)), dma((2, pl_z)),
        dma((2, pl_lat + pl_z)), dma((2, pl_lat + pl_z)),
        dma((pl_lat + pl_z,)), dma((pl_lat + pl_z,)),
    ]
    out, gtok, fin, small = pl.pallas_call(
        functools.partial(kernel, dims),
        out_shape=[
            jax.ShapeDtypeStruct((count, feats), BF16),
            jax.ShapeDtypeStruct((count, feats), BF16),
            jax.ShapeDtypeStruct((2, 2 * feats, feats), BF16),
            jax.ShapeDtypeStruct((8, feats), F32),
        ],
        in_specs=[hbm] * 7 + [sm],
        out_specs=[vm] * 4,
        scratch_shapes=scratch,
        compiler_params=pltpu.CompilerParams(
            collective_id=0, has_side_effects=True, vmem_limit_bytes=60 * 1024 * 1024
        ),
    )(
        tokens.reshape(count, feats), cotangent.reshape(count, feats), wq, wk, wv, wo,
        norm_gain.reshape(1, feats), logit_scale,
    )
    if not reduce_here:
        fin, small = lax.psum((fin, small), ("lat", "lon"))
    weight = jax.ShapeDtypeStruct((feats, feats), F32)
    tile = jax.ShapeDtypeStruct((count, feats), BF16)
    done = pl.pallas_call(
        finish,
        out_shape=[
            tile, tile, weight, weight, weight, weight,
            jax.ShapeDtypeStruct((1, feats), F32), jax.ShapeDtypeStruct((1, HEADS), F32),
        ],
        in_specs=[vm] * 4,
        out_specs=[hbm] * 8,
        scratch_shapes=[V((feats, feats), F32)] * 4
        + [V((1, feats), F32), V((1, HEADS), F32), dma((8,))],
        compiler_params=pltpu.CompilerParams(vmem_limit_bytes=60 * 1024 * 1024),
    )(fin, small, out, gtok)
    return (
        done[0].reshape(rows, cols, feats), done[1].reshape(rows, cols, feats),
        *done[2:6], done[6].reshape(feats), done[7].reshape(HEADS),
    )


def solution(mesh):
    n_lat, n_lon = mesh.shape["lat"], mesh.shape["lon"]

    def run(tokens, *rest):
        dims = (n_lat, n_lon, tokens.shape[0], tokens.shape[1])
        return local(dims, tokens, *rest)

    return jax.shard_map(
        run,
        mesh=mesh,
        in_specs=(P("lat", "lon", None), P("lat", "lon", None), P(), P(), P(), P(), P(), P()),
        out_specs=(P("lat", "lon", None), P("lat", "lon", None), P(), P(), P(), P(), P(), P()),
        check_vma=False,
    )
```

```python
import functools

import jax
import jax.numpy as jnp
from jax import lax
from jax.experimental import pallas as pl
from jax.experimental.pallas import tpu as pltpu
from jax.sharding import PartitionSpec as P

HEADS = 8
REACH = 6
EPS = 1e-05
FLOOR = 0.5
BLOCK = 8
MESH = pl.DeviceIdType.MESH
F32 = jnp.float32
BF16 = jnp.bfloat16
OFFSETS = ((0, -1), (0, 1), (-1, 0), (1, 0), (-1, -1), (-1, 1), (1, -1), (1, 1))


def dot_nn(a, b):
    return lax.dot_general(a, b, (((1,), (0,)), ((), ())), preferred_element_type=F32)


def dot_nt(a, b):
    return lax.dot_general(a, b, (((1,), (1,)), ((), ())), preferred_element_type=F32)


def dot_tn(a, b):
    return lax.dot_general(a, b, (((0,), (0,)), ((), ())), preferred_element_type=F32)


def group_mean(x, ones):
    return dot_nn(x.astype(BF16), ones)


def kernel(
    dims,
    tok_in, cot_in, wq_in, wk_in, wv_in, wo_in, gain_in, scale,
    out, gtok, fin_out, small_out,
    tok, cot, wq, wk, wv, wo, gain,
    win, kbuf, vbuf, kraw, kinv, xhat, nrm, qu, qraw, qinv, ag, qe, ge, sc, dp, pb, db, dk, dv, dq, att,
    wg, ngs, ngo, rback, rcore, s1, rlat, s2, rz, fin, small, smcore, smlat, smz,
    load_sem, hs, hr, bs, br, cs, cr, ls, lr, zs, zr, gs, gr, ts, tr,
):
    n_lat, n_lon, rows, cols = dims
    nz = n_lon // 2
    count = rows * cols
    halo = REACH * cols
    tall = count + 2 * halo
    feats = tok_in.shape[1]
    head = feats // HEADS
    nb = BLOCK * cols
    wrows = (BLOCK + 2 * REACH) * cols
    keys = 3 * wrows
    reduce_here = 2 * feats % (2 * n_lat * nz * 16) == 0
    a = lax.axis_index("lat")
    b = lax.axis_index("lon")
    core = lax.rem(b, 2)
    z = b // 2
    sibling = (a, b + 1 - 2 * core)

    def lat_peer(j):
        return (lax.rem(a + j, n_lat), b)

    def z_peer(j):
        return (a, lax.rem(z + j, nz) * 2 + core)

    def near(da, db):
        return (lax.rem(a + da + n_lat, n_lat), lax.rem(b + db + n_lon, n_lon))

    peers = [near(*o) for o in OFFSETS]
    if reduce_here:
        peers += [sibling] + [lat_peer(j) for j in range(1, n_lat)] + [z_peer(j) for j in range(1, nz)]
    barrier = pltpu.get_barrier_semaphore()
    for p in peers:
        pl.semaphore_signal(barrier, inc=1, device_id=p, device_id_type=MESH)
    loads = []
    for src, dst in (
        (tok_in, tok), (wk_in, wk), (wv_in, wv), (gain_in, gain), (wq_in, wq), (cot_in, cot), (wo_in, wo)
    ):
        c = pltpu.make_async_copy(src, dst, load_sem.at[len(loads)])
        c.start()
        loads.append(c)
    pl.semaphore_wait(barrier, len(peers))

    def send(src, dst, s, r, to):
        c = pltpu.make_async_remote_copy(
            src_ref=src, dst_ref=dst, send_sem=s, recv_sem=r, device_id=to, device_id_type=MESH
        )
        c.start()
        return c

    def strip(da):
        return {0: (0, halo, count), 1: (count - halo, 0, halo), -1: (0, halo + count, halo)}[da]

    halos = []
    for i, (da, d) in enumerate(OFFSETS):
        src, dst, n = strip(da)
        halos.append(
            send(
                tok_in.at[pl.ds(src, n)], win.at[pl.ds((1 - d) * tall + dst, n)],
                hs.at[i], hr.at[i], near(da, d),
            )
        )

    lane = lax.broadcasted_iota(jnp.int32, (1, feats), 1) // head
    gi = lax.broadcasted_iota(jnp.int32, (feats, feats), 0) // head
    gj = lax.broadcasted_iota(jnp.int32, (feats, feats), 1) // head
    ones = jnp.where(gi == gj, 1.0 / head, 0.0).astype(BF16)

    def norm_parts(x):
        x = x.astype(F32)
        sh = x - jnp.mean(x, axis=-1, keepdims=True)
        rstd = lax.rsqrt(jnp.mean(sh * sh, axis=-1, keepdims=True) + EPS)
        return sh, rstd

    def project(x, lo, n):
        sh, rstd = norm_parts(x)
        xh = sh * rstd
        xhat[pl.ds(lo, n)] = xh
        nn = (gain[...] * xh).astype(BF16)
        nrm[pl.ds(lo, n)] = nn
        kr = dot_nn(nn, wk[...])
        kraw[pl.ds(lo, n)] = kr
        inv = lax.rsqrt(group_mean(kr * kr, ones) + FLOOR)
        kinv[pl.ds(lo, n)] = inv
        kbuf[pl.ds(lo, n)] = (kr * inv).astype(BF16)
        vbuf[pl.ds(lo, n)] = dot_nn(nn, wv[...]).astype(BF16)

    mine = tall + halo
    wide = jnp.zeros((1, feats), F32)
    for h in range(HEADS):
        wide = jnp.where(lane == h, scale[h] * (1.0 / head), wide)
    for c in loads:
        c.wait()
    project(tok[...], mine, count)
    qr = dot_nn(nrm[pl.ds(mine, count)], wq[...])
    qraw[...] = qr
    inv = lax.rsqrt(group_mean(qr * qr, ones) + FLOOR)
    qinv[...] = inv
    qu[...] = (qr * inv).astype(BF16)
    ag[...] = dot_nt(cot[...], wo[...]).astype(BF16)
    dk[...] = jnp.zeros_like(dk)
    dv[...] = jnp.zeros_like(dv)
    small[...] = jnp.zeros_like(small)
    for c in halos:
        c.wait()
    project(win[pl.ds(0, tall)], 0, tall)
    project(win[pl.ds(2 * tall, tall)], 2 * tall, tall)
    project(win[pl.ds(tall, halo)], tall, halo)
    project(win[pl.ds(tall + halo + count, halo)], tall + halo + count, halo)

    total_rows = n_lat * rows
    qi = lax.broadcasted_iota(jnp.int32, (nb, keys), 0)
    ki = lax.broadcasted_iota(jnp.int32, (nb, keys), 1)
    tile = (ki >= wrows).astype(jnp.int32) + (ki >= 2 * wrows).astype(jnp.int32)
    within = ki - tile * wrows
    row_gap = within // cols - REACH - qi // cols
    col_gap = lax.rem(within, cols) + tile * cols - cols - lax.rem(qi, cols)
    close = (jnp.abs(row_gap) <= REACH) & (jnp.abs(col_gap) <= REACH)
    krow = within // cols - REACH + a * rows

    def block(i, carried):
        q0 = pl.multiple_of(i * nb, nb)
        qb = qu[pl.ds(q0, nb)]
        gb = ag[pl.ds(q0, nb)]
        for h in range(HEADS):
            qe[pl.ds(h * nb, nb)] = jnp.where(lane == h, qb, jnp.zeros_like(qb))
            ge[pl.ds(h * nb, nb)] = jnp.where(lane == h, gb, jnp.zeros_like(gb))
        starts = [pl.multiple_of(t * tall + i * nb, 16) for t in range(3)]
        kw = jnp.concatenate([kbuf[pl.ds(s, wrows)] for s in starts], axis=0)
        vw = jnp.concatenate([vbuf[pl.ds(s, wrows)] for s in starts], axis=0)
        sc[...] = dot_nt(qe[...], kw)
        dp[...] = dot_nt(ge[...], vw)
        gr_row = krow + i * BLOCK
        seen = jnp.where(close & (gr_row >= 0) & (gr_row < total_rows), 1.0, 0.0)
        for h in range(HEADS):
            part = pl.ds(h * nb, nb)
            s = sc[part]
            e = jnp.exp(s * (scale[h] * (1.0 / head))) * seen
            p = e * (1.0 / jnp.sum(e, axis=1, keepdims=True))
            pb[part] = p.astype(BF16)
            t = dp[part]
            g = p * (t - jnp.sum(p * t, axis=1, keepdims=True))
            db[part] = g.astype(BF16)
            tot = jnp.sum(jnp.sum(g * s, axis=1, keepdims=True), axis=0, keepdims=True)
            small[1:2, :] = small[1:2, :] + jnp.where(lane == h, tot * (1.0 / head), 0.0)
        o = dot_nn(pb[...], vw)
        u = dot_nn(db[...], kw)
        oa = jnp.zeros((nb, feats), F32)
        ua = jnp.zeros((nb, feats), F32)
        for h in range(HEADS):
            oa = jnp.where(lane == h, o[h * nb : (h + 1) * nb], oa)
            ua = jnp.where(lane == h, u[h * nb : (h + 1) * nb], ua)
        att[pl.ds(q0, nb)] = oa.astype(BF16)
        dq[pl.ds(q0, nb)] = ua
        kg = dot_tn(db[...], qe[...])
        vg = dot_tn(pb[...], ge[...])
        for t in range(3):
            part = pl.ds(starts[t], wrows)
            dk[part] = dk[part] + kg[t * wrows : (t + 1) * wrows]
            dv[part] = dv[part] + vg[t * wrows : (t + 1) * wrows]
        return carried

    lax.fori_loop(0, rows // BLOCK, block, 0)

    def head_back(raw, inv, g):
        return inv * (g - raw * (inv * inv) * group_mean(g * raw, ones))

    half, quarter, last = wg.shape[1] // 2, rlat.shape[2], rz.shape[2]
    chunks = range(wg.shape[0])
    my_half = pl.multiple_of(core * half, 16)
    block_lo = pl.multiple_of(my_half + a * quarter, 16)
    leaf_lo = pl.multiple_of(block_lo + z * last, 16)

    def core_send(k):
        lo = pl.multiple_of((1 - core) * half, 16)
        return send(wg.at[k, pl.ds(lo, half)], rcore.at[k], cs.at[k], cr.at[k], sibling)

    def lat_send(k):
        s1[k] = (wg[k, pl.ds(my_half, half)].astype(F32) + rcore[k].astype(F32)).astype(BF16)
        sent = []
        for j in range(1, n_lat):
            to = lat_peer(j)
            lo = pl.multiple_of(to[0] * quarter, 16)
            sent.append(
                send(s1.at[k, pl.ds(lo, quarter)], rlat.at[k, j - 1], ls.at[k, j], lr.at[k, j], to)
            )
        return sent

    def z_send(k):
        acc = s1[k, pl.ds(pl.multiple_of(a * quarter, 16), quarter)].astype(F32)
        for j in range(1, n_lat):
            acc = acc + rlat[k, j - 1].astype(F32)
        s2[k] = acc.astype(BF16)
        sent = []
        for j in range(1, nz):
            to = z_peer(j)
            lo = pl.multiple_of((to[1] // 2) * last, 16)
            sent.append(send(s2.at[k, pl.ds(lo, last)], rz.at[k, j - 1], zs.at[k, j], zr.at[k, j], to))
        return sent

    def z_spread(k):
        acc = s2[k, pl.ds(pl.multiple_of(z * last, 16), last)].astype(F32)
        for j in range(1, nz):
            acc = acc + rz[k, j - 1].astype(F32)
        leaf = pl.ds(leaf_lo, last)
        fin[k, leaf] = acc.astype(BF16)
        return [
            send(fin.at[k, leaf], fin.at[k, leaf], gs.at[k, j], gr.at[k, j], z_peer(j))
            for j in range(1, nz)
        ]

    def lat_spread(k):
        mid = pl.ds(block_lo, quarter)
        return [
            send(fin.at[k, mid], fin.at[k, mid], gs.at[k, nz + j], gr.at[k, nz + j], lat_peer(j))
            for j in range(1, n_lat)
        ]

    def core_spread(k, j):
        lo = pl.multiple_of(my_half + lax.rem(a - j + n_lat, n_lat) * quarter, 16)
        rows_j, sem = pl.ds(lo, quarter), nz + n_lat + j
        return send(fin.at[k, rows_j], fin.at[k, rows_j], gs.at[k, sem], gr.at[k, sem], sibling)

    def forward(k, copies):
        sent = []
        for j, c in enumerate(copies):
            c.wait()
            sent.append(core_spread(k, j + 1))
        return sent

    def done(copies):
        for c in copies:
            c.wait()

    dqr = head_back(qraw[...], qinv[...], dq[...] * wide).astype(BF16)
    wg[0, pl.ds(0, feats)] = dot_tn(nrm[pl.ds(mine, count)], dqr).astype(BF16)
    wg[0, pl.ds(feats, feats)] = dot_tn(att[...], cot[...]).astype(BF16)
    if reduce_here:
        c0 = [core_send(0)]
    dkr = head_back(kraw[...], kinv[...], dk[...] * wide).astype(BF16)
    dvb = dv[...].astype(BF16)
    wg[1, pl.ds(0, feats)] = dot_tn(nrm[...], dkr).astype(BF16)
    wg[1, pl.ds(feats, feats)] = dot_tn(nrm[...], dvb).astype(BF16)
    if reduce_here:
        c1 = [core_send(1)]
        done(c0)
        c0 = lat_send(0)
    ng = dot_nt(dkr, wk[...]) + dot_nt(dvb, wv[...])
    ngs[...] = ng.astype(BF16)
    backs = []
    for i, (da, d) in enumerate(OFFSETS):
        _, _, n = strip(da)
        src = {0: halo, -1: 0, 1: halo + count}[da]
        backs.append(
            send(
                ngs.at[pl.ds((1 + d) * tall + src, n)], rback.at[i, pl.ds(0, n)],
                bs.at[i], br.at[i], near(da, d),
            )
        )
    if reduce_here:
        done(c1)
        c1 = lat_send(1)
    from_q = dot_nt(dqr, wq[...])
    ngo[...] = ng[mine : mine + count] + from_q
    own_hat = xhat[pl.ds(mine, count)]
    small[0:1, :] = jnp.sum(ng * xhat[...], axis=0, keepdims=True) + jnp.sum(
        from_q * own_hat, axis=0, keepdims=True
    )
    if reduce_here:
        m = [send(small, smcore, ts.at[0], tr.at[0], sibling)]
        done(c0)
        c0 = z_send(0)
        done(m)
        smlat[pl.ds(a, 1)] = (small[...] + smcore[...])[None]
        m = [send(smlat.at[a], smlat.at[a], ts.at[j], tr.at[j], lat_peer(j)) for j in range(1, n_lat)]
    out[...] = (tok[...].astype(F32) + dot_nn(att[...], wo[...])).astype(BF16)
    if reduce_here:
        done(c1)
        c1 = z_send(1)
        done(c0)
        c0 = z_spread(0)
        done(m)
        acc = smlat[0]
        for j in range(1, n_lat):
            acc = acc + smlat[j]
        smz[pl.ds(z, 1)] = acc[None]
        m = [
            send(smz.at[z], smz.at[z], ts.at[n_lat + j], tr.at[n_lat + j], z_peer(j))
            for j in range(1, nz)
        ]
        done(c1)
        c1 = z_spread(1)
        done(c0)
        c0 = lat_spread(0)
        own0 = core_spread(0, 0)
        done(c1)
        c1 = lat_spread(1)
        own1 = core_spread(1, 0)
    done(backs)
    ngo[...] = ngo[...] + rback[0].astype(F32) + rback[1].astype(F32)
    for da, lo in ((-1, 0), (1, count - halo)):
        part = pl.ds(lo, halo)
        add = ngo[part]
        for i, o in enumerate(OFFSETS):
            if o[0] == -da:
                add = add + rback[i, pl.ds(0, halo)].astype(F32)
        ngo[part] = add
    sh, rstd = norm_parts(tok[...])
    g = ngo[...] * gain[...]
    tg = rstd * (
        g
        - jnp.mean(g, axis=-1, keepdims=True)
        - own_hat * jnp.mean(g * own_hat, axis=-1, keepdims=True)
    )
    gtok[...] = (cot[...].astype(F32) + tg).astype(BF16)
    if reduce_here:
        c0 = forward(0, c0) + [own0]
        c1 = forward(1, c1) + [own1]
        done(m)
        acc = smz[0]
        for j in range(1, nz):
            acc = acc + smz[j]
        small_out[...] = acc
        done(c0)
        fin_out[0] = fin[0]
        done(c1)
        fin_out[1] = fin[1]
    else:
        fin_out[...] = wg[...]
        small_out[...] = small[...]


def finish(fin, small, out, gtok, *refs):
    results, staged, sem = refs[:8], refs[8:14], refs[14]
    feats = fin.shape[2]
    pending = []

    def store(src, dst):
        c = pltpu.make_async_copy(src, dst, sem.at[len(pending)])
        c.start()
        pending.append(c)

    store(out, results[0])
    store(gtok, results[1])
    for n, (k, lo) in enumerate(((0, 0), (1, 0), (1, feats), (0, feats))):
        staged[n][...] = fin[k, pl.ds(lo, feats)].astype(F32)
        store(staged[n], results[2 + n])
    staged[4][...] = small[0:1, :]
    store(staged[4], results[6])
    lane = lax.broadcasted_iota(jnp.int32, (feats, HEADS), 0)
    col = lax.broadcasted_iota(jnp.int32, (feats, HEADS), 1)
    pick = jnp.where(lane == col * (feats // HEADS), 1.0, 0.0)
    staged[5][...] = lax.dot_general(
        small[...], pick, (((1,), (0,)), ((), ())), precision=lax.Precision.HIGHEST,
        preferred_element_type=F32,
    )[1:2, :]
    store(staged[5], results[7])
    for c in pending:
        c.wait()


def local(dims, tokens, cotangent, wq, wk, wv, wo, norm_gain, logit_scale):
    n_lat, n_lon, rows, cols = dims
    nz = n_lon // 2
    feats = tokens.shape[-1]
    head = feats // HEADS
    count = rows * cols
    halo = REACH * cols
    window = 3 * (count + 2 * halo)
    nb = BLOCK * cols * HEADS
    keys = 3 * (BLOCK + 2 * REACH) * cols
    reduce_here = 2 * feats % (2 * n_lat * nz * 16) == 0
    half = feats
    quarter = half // n_lat if reduce_here else 16
    last = quarter // nz if reduce_here else 16
    pl_lat = n_lat if reduce_here else 2
    pl_z = nz if reduce_here else 2
    vm = pl.BlockSpec(memory_space=pltpu.VMEM)
    sm = pl.BlockSpec(memory_space=pltpu.SMEM)
    hbm = pl.BlockSpec(memory_space=pltpu.HBM)
    dma = pltpu.SemaphoreType.DMA
    V = pltpu.VMEM
    square = V((feats, feats), BF16)
    scratch = [
        V((count, feats), BF16), V((count, feats), BF16), square, square, square, square,
        V((1, feats), F32),
        V((window, feats), BF16), V((window, feats), BF16), V((window, feats), BF16),
        V((window, feats), F32), V((window, feats), F32), V((window, feats), F32),
        V((window, feats), BF16),
        V((count, feats), BF16), V((count, feats), F32), V((count, feats), F32),
        V((count, feats), BF16),
        V((nb, feats), BF16), V((nb, feats), BF16),
        V((nb, keys), F32), V((nb, keys), F32), V((nb, keys), BF16), V((nb, keys), BF16),
        V((window, feats), F32), V((window, feats), F32), V((count, feats), F32),
        V((count, feats), BF16),
        V((2, 2 * feats, feats), BF16), V((window, feats), BF16), V((count, feats), F32),
        V((8, count, feats), BF16),
        V((2, half, feats), BF16), V((2, half, feats), BF16),
        V((2, pl_lat - 1, quarter, feats), BF16), V((2, quarter, feats), BF16),
        V((2, pl_z - 1, last, feats), BF16), V((2, 2 * feats, feats), BF16),
        V((8, feats), F32), V((8, feats), F32), V((pl_lat, 8, feats), F32), V((pl_z, 8, feats), F32),
        dma((7,)),
        dma((8,)), dma((8,)), dma((8,)), dma((8,)), dma((2,)), dma((2,)),
        dma((2, pl_lat)), dma((2, pl_lat)), dma((2, pl_z)), dma((2, pl_z)),
        dma((2, 2 * pl_lat + pl_z)), dma((2, 2 * pl_lat + pl_z)),
        dma((pl_lat + pl_z,)), dma((pl_lat + pl_z,)),
    ]
    out, gtok, fin, small = pl.pallas_call(
        functools.partial(kernel, dims),
        out_shape=[
            jax.ShapeDtypeStruct((count, feats), BF16),
            jax.ShapeDtypeStruct((count, feats), BF16),
            jax.ShapeDtypeStruct((2, 2 * feats, feats), BF16),
            jax.ShapeDtypeStruct((8, feats), F32),
        ],
        in_specs=[hbm] * 7 + [sm],
        out_specs=[vm] * 4,
        scratch_shapes=scratch,
        compiler_params=pltpu.CompilerParams(
            collective_id=0, has_side_effects=True, vmem_limit_bytes=60 * 1024 * 1024
        ),
    )(
        tokens.reshape(count, feats), cotangent.reshape(count, feats), wq, wk, wv, wo,
        norm_gain.reshape(1, feats), logit_scale,
    )
    if not reduce_here:
        fin, small = lax.psum((fin, small), ("lat", "lon"))
    weight = jax.ShapeDtypeStruct((feats, feats), F32)
    tile = jax.ShapeDtypeStruct((count, feats), BF16)
    done = pl.pallas_call(
        finish,
        out_shape=[
            tile, tile, weight, weight, weight, weight,
            jax.ShapeDtypeStruct((1, feats), F32), jax.ShapeDtypeStruct((1, HEADS), F32),
        ],
        in_specs=[vm] * 4,
        out_specs=[hbm] * 8,
        scratch_shapes=[V((feats, feats), F32)] * 4
        + [V((1, feats), F32), V((1, HEADS), F32), dma((8,))],
        compiler_params=pltpu.CompilerParams(vmem_limit_bytes=60 * 1024 * 1024),
    )(fin, small, out, gtok)
    return (
        done[0].reshape(rows, cols, feats), done[1].reshape(rows, cols, feats),
        *done[2:6], done[6].reshape(feats), done[7].reshape(HEADS),
    )


def solution(mesh):
    n_lat, n_lon = mesh.shape["lat"], mesh.shape["lon"]

    def run(tokens, *rest):
        dims = (n_lat, n_lon, tokens.shape[0], tokens.shape[1])
        return local(dims, tokens, *rest)

    return jax.shard_map(
        run,
        mesh=mesh,
        in_specs=(P("lat", "lon", None), P("lat", "lon", None), P(), P(), P(), P(), P(), P()),
        out_specs=(P("lat", "lon", None), P("lat", "lon", None), P(), P(), P(), P(), P(), P()),
        check_vma=False,
    )
```
